32 devices in a mesh: ens: 2 (over x), dom: 8 (over z, y), lat: 2 (over core).
Axes of the slice: x: 2, y: 2, z: 4, core: 2. Of those that a mesh axis runs over, the one named last changes fastest.
Arguments:
- node_lat: bfloat16 [5120, 512], P(('ens', 'dom'), 'lat'), parts along dimension 0, may hold values from -6 to 6
- edge_lat: bfloat16 [40960, 512], P(('ens', 'dom'), 'lat'), parts along dimension 0, may hold values from -6 to 6
- halo_rows: int32 [16, 8, 80], P('ens'), parts along dimension 0, may hold values from 0 to 320, as said below
- edge_sender: int32 [40960], P(('ens', 'dom')), parts along dimension 0, may hold values from 0 to 959, as said below
- edge_receiver: int32 [40960], P(('ens', 'dom')), parts along dimension 0, may hold values from 0 to 319, as said below
- edge_w_in: bfloat16 [1536, 512], replicated, may hold values from -0.15625 to 0.15625
- edge_b_in: float32 [512], replicated, may hold values from -3 to 3
- edge_w_out: bfloat16 [512, 512], replicated, may hold values from -0.25 to 0.25
- edge_b_out: float32 [512], replicated, may hold values from -4 to 4
- edge_gain: float32 [512], replicated, may hold values from 0.1 to 1.9
- edge_shift: float32 [512], replicated, may hold values from -3 to 3
- node_w_in: bfloat16 [1024, 512], replicated, may hold values from -0.1875 to 0.1875
- node_b_in: float32 [512], replicated, may hold values from -3 to 3
- node_w_out: bfloat16 [512, 512], replicated, may hold values from -0.25 to 0.25
- node_b_out: float32 [512], replicated, may hold values from -4 to 4
- node_gain: float32 [512], replicated, may hold values from 0.1 to 1.9
- node_shift: float32 [512], replicated, may hold values from -3 to 3
- node_ct: bfloat16 [5120, 512], P(('ens', 'dom'), 'lat'), parts along dimension 0, may hold values from -6 to 6
- edge_ct: bfloat16 [40960, 512], P(('ens', 'dom'), 'lat'), parts along dimension 0, may hold values from -6 to 6
Outputs:
- node_new: bfloat16 [5120, 512], P(('ens', 'dom'), 'lat'), parts along dimension 0
- edge_new: bfloat16 [40960, 512], P(('ens', 'dom'), 'lat'), parts along dimension 0
- node_grad: float32 [5120, 512], P(('ens', 'dom'), 'lat'), parts along dimension 0
- edge_grad: float32 [40960, 512], P(('ens', 'dom'), 'lat'), parts along dimension 0
The draws below stay inside these ranges and needn't reach their ends.
There are 2 independent parts, one for each index of `ens`. The reference program is written for one: setup_inputs(seed, part) draws one part's arguments, and reference() takes and returns one part's arrays. A program takes and returns all parts, laid end to end along the dimension named above; an argument that names none is the same for every part. Nothing has to cross between parts.
Inputs may be any that keep to these rules, and one draw needn't show every extreme that they name: halo_rows[p, q] lists distinct rows of partition p read by edges of partition q: its used slots come first, and every empty slot holds 320. The list of a partition to itself is empty, every other list holds one or more rows, and the list of p to p + 1 (cyclically) is full. `edge_sender`: A value s below 320 is a row of the edge's own partition p; otherwise s = 320 + q * 80 + k names used slot k of halo_rows[q, p]. `edge_receiver`: the edges of a partition fall into 2 aligned blocks of 1280 rows, and the receivers of block j are rows j * 160 to (j + 1) * 160 - 1.
All inputs are finite; a program needn't handle non-finite values.
Results may differ from the reference program's by a relative error of at most 0.012.
Values may be sent and summed in bfloat16 or wider, within the bound.
A program may use at most 64 MiB of HBM per device.

```python
import jax
import jax.numpy as jnp
from jax import lax

LATENT = 512
UNITS = 512
NODE_DEV = 320
EDGE_DEV = 2560
SLOTS = 80
NODES = 2560
EDGES = 20480
EDGE_BLOCK = 1280
NODE_BLOCK = 160
N_DOM = 8


def graph_layout(key):
    key_count, key_perm, key_pick, key_local, key_kind, key_recv = jax.random.split(key, 6)
    eye_rows = jnp.arange(N_DOM)
    counts = jax.random.randint(key_count, (N_DOM, N_DOM), 1, SLOTS + 1)
    full_peer = (eye_rows + 1) % N_DOM
    counts = counts.at[eye_rows, full_peer].set(SLOTS)
    counts = jnp.where(eye_rows[:, None] == eye_rows[None, :], 0, counts)
    perm_keys = jax.random.split(key_perm, N_DOM * N_DOM)
    chosen = jax.vmap(lambda single: jax.random.permutation(single, NODE_DEV)[:SLOTS])(perm_keys)
    chosen = chosen.reshape(N_DOM, N_DOM, SLOTS)
    filled = jnp.arange(SLOTS)[None, None, :] < counts[:, :, None]
    halo_table = jnp.where(filled, chosen, NODE_DEV).astype(jnp.int32)
    usable = jnp.transpose(filled, (1, 0, 2)).reshape(N_DOM, N_DOM * SLOTS)
    running = jnp.cumsum(usable.astype(jnp.int32), axis=1)
    totals = running[:, -1]
    picked = jax.random.randint(key_pick, (N_DOM, EDGE_DEV), 0, totals[:, None])
    slot_index = jax.vmap(lambda running_row, wanted: jnp.searchsorted(running_row, wanted, side='right'))(running, picked)
    local_row = jax.random.randint(key_local, (N_DOM, EDGE_DEV), 0, NODE_DEV)
    remote = jax.random.randint(key_kind, (N_DOM, EDGE_DEV), 0, 2) == 1
    sender = jnp.where(remote, NODE_DEV + slot_index, local_row)
    last_slot = NODE_DEV + (eye_rows - 1) % N_DOM * SLOTS + SLOTS - 1
    sender = sender.at[:, 0].set(last_slot)
    block_start = jnp.arange(EDGE_DEV) // EDGE_BLOCK * NODE_BLOCK
    receiver = block_start[None, :] + jax.random.randint(key_recv, (N_DOM, EDGE_DEV), 0, NODE_BLOCK)
    return (halo_table, sender.reshape(-1).astype(jnp.int32), receiver.reshape(-1).astype(jnp.int32))


def draw_halo_rows(key, part):
    return graph_layout(key)[0]


def draw_edge_sender(key, part):
    return graph_layout(key)[1]


def draw_edge_receiver(key, part):
    return graph_layout(key)[2]


def levels(rng, shape, cuts, low, largest):
    def one(position, shards_of):
        draws = jax.random.uniform(jax.random.fold_in(jax.random.fold_in(rng, 6), position), (shards_of,), jnp.float32, low / len(cuts), largest / len(cuts))
        return jnp.repeat(jnp.exp(draws), shape[position] // shards_of).reshape((-1,) + (1,) * (len(shape) - position - 1))

    loudness = one(*cuts[0])
    for cut in cuts[1:]:
        loudness = loudness * one(*cut)
    return loudness


def scatter_about(key, extent, scale, bound, cuts=(), kind=jnp.bfloat16):
    drawn = jax.random.normal(key, extent, jnp.float32) * scale
    if len(cuts) > 0:
        drawn = levels(key, extent, cuts, -0.22, 0.18) * drawn
    return jnp.clip(drawn, min=-bound, max=bound).astype(kind)


def setup_inputs(seed: int = 0, part: int = 0) -> dict:
    key_list = jax.random.split(jax.random.key(seed), 20)
    part_splits = jax.random.split(jax.random.fold_in(key_list[19], part), 20)
    return {
        "node_lat": scatter_about(part_splits[0], (NODES, LATENT), 1.0, 6.0, ((0, 8), (1, 2))),
        "edge_lat": scatter_about(part_splits[1], (EDGES, LATENT), 1.0, 6.0, ((0, 8), (1, 2))),
        "halo_rows": draw_halo_rows(jax.random.fold_in(jax.random.fold_in(key_list[19], part), 71), part),
        "edge_sender": draw_edge_sender(jax.random.fold_in(jax.random.fold_in(key_list[19], part), 71), part),
        "edge_receiver": draw_edge_receiver(jax.random.fold_in(jax.random.fold_in(key_list[19], part), 71), part),
        "edge_w_in": scatter_about(key_list[5], (3 * LATENT, UNITS), (3 * LATENT) ** -0.5, 0.15625),
        "edge_b_in": scatter_about(key_list[6], (UNITS,), 0.5, 3.0, (), jnp.float32),
        "edge_w_out": scatter_about(key_list[7], (UNITS, LATENT), UNITS ** -0.5, 0.25),
        "edge_b_out": scatter_about(key_list[8], (LATENT,), 1.0, 4.0, (), jnp.float32),
        "edge_gain": jnp.clip(1.0 + 0.18 * jax.random.normal(key_list[9], (LATENT,), jnp.float32), 0.1, 1.9),
        "edge_shift": scatter_about(key_list[10], (LATENT,), 0.5, 3.0, (), jnp.float32),
        "node_w_in": scatter_about(key_list[11], (2 * LATENT, UNITS), (2 * LATENT) ** -0.5, 0.1875),
        "node_b_in": scatter_about(key_list[12], (UNITS,), 0.5, 3.0, (), jnp.float32),
        "node_w_out": scatter_about(key_list[13], (UNITS, LATENT), UNITS ** -0.5, 0.25),
        "node_b_out": scatter_about(key_list[14], (LATENT,), 1.0, 4.0, (), jnp.float32),
        "node_gain": jnp.clip(1.0 + 0.18 * jax.random.normal(key_list[15], (LATENT,), jnp.float32), 0.1, 1.9),
        "node_shift": scatter_about(key_list[16], (LATENT,), 0.5, 3.0, (), jnp.float32),
        "node_ct": scatter_about(part_splits[17], (NODES, LATENT), 1.0, 6.0, ((0, 8), (1, 2))),
        "edge_ct": scatter_about(part_splits[18], (EDGES, LATENT), 1.0, 6.0, ((0, 8), (1, 2))),
    }


def layer_block(inputs, w_in, b_in, w_out, b_out, scales, offsets):
    before = jnp.dot(inputs, w_in, preferred_element_type=jnp.float32) + b_in
    active = jax.nn.silu(before).astype(jnp.bfloat16)
    output = jnp.dot(active, w_out, preferred_element_type=jnp.float32) + b_out
    average = lax.optimization_barrier(jnp.mean(output, axis=-1, keepdims=True))
    centred = output - average
    variance = lax.optimization_barrier(jnp.mean(centred * centred, axis=-1, keepdims=True))
    return centred * lax.rsqrt(variance + 1e-05) * scales + offsets

def process(edge_full, sender_bf, node_full, receiver, edge_params, node_params):
    receiver_bf = jnp.take(node_full, receiver, axis=0).astype(jnp.bfloat16)
    edge_input = jnp.concatenate([edge_full.astype(jnp.bfloat16), sender_bf, receiver_bf], axis=1)
    edge_new = (edge_full + layer_block(edge_input, edge_params[0], edge_params[1], edge_params[2], edge_params[3], edge_params[4], edge_params[5])).astype(jnp.bfloat16)
    summed = jax.ops.segment_sum(edge_new.astype(jnp.float32), receiver, num_segments=node_full.shape[0])
    node_input = jnp.concatenate([node_full.astype(jnp.bfloat16), summed.astype(jnp.bfloat16)], axis=1)
    node_new = (node_full + layer_block(node_input, node_params[0], node_params[1], node_params[2], node_params[3], node_params[4], node_params[5])).astype(jnp.bfloat16)
    return (edge_new, node_new)

def reference(node_lat, edge_lat, halo_rows, edge_sender, edge_receiver, edge_w_in, edge_b_in, edge_w_out, edge_b_out, edge_gain, edge_shift, node_w_in, node_b_in, node_w_out, node_b_out, node_gain, node_shift, node_ct, edge_ct):
    edge_params = (edge_w_in, edge_b_in, edge_w_out, edge_b_out, edge_gain, edge_shift)
    node_params = (node_w_in, node_b_in, node_w_out, node_b_out, node_gain, node_shift)
    part_of_edge = (jnp.arange(EDGES) // EDGE_DEV).astype(jnp.int32)
    direct = edge_sender < NODE_DEV
    offset = jnp.maximum(edge_sender - NODE_DEV, 0).astype(jnp.int32)
    source = offset // SLOTS
    remote_row = halo_rows[source, part_of_edge, offset % SLOTS]
    sender_node = jnp.where(direct, part_of_edge * NODE_DEV + edge_sender, source * NODE_DEV + remote_row).astype(jnp.int32)
    receiver_node = (part_of_edge * NODE_DEV + edge_receiver).astype(jnp.int32)

    def forward(node_full, edge_full):
        sender_bf = jnp.take(node_full, sender_node, axis=0).astype(jnp.bfloat16)
        return process(edge_full, sender_bf, node_full, receiver_node, edge_params, node_params)
    outputs, pullback = jax.vjp(forward, node_lat.astype(jnp.float32), edge_lat.astype(jnp.float32))
    edge_new, node_new = outputs
    node_grad, edge_grad = pullback((edge_ct, node_ct))
    return (node_new, edge_new, node_grad, edge_grad)
```

```python
import functools

import jax
import jax.numpy as jnp
from jax import lax
from jax.experimental import pallas as pl
from jax.experimental.pallas import tpu as pltpu
from jax.sharding import PartitionSpec as P

F32 = jnp.float32
BF16 = jnp.bfloat16


def mm(a, b):
    return jnp.dot(a, b, preferred_element_type=F32)


def mm_t(a, b):
    return lax.dot_general(a, b, (((1,), (1,)), ((), ())), preferred_element_type=F32)


def one_hot(match):
    return jnp.where(match, 1.0, 0.0).astype(BF16)


def column(row):
    return jnp.broadcast_to(row, (128, row.shape[1])).T


def across(col, depth):
    return one_hot(lax.broadcasted_iota(jnp.int32, (col.shape[0], depth), 1) == col[:, :1])


def down(row, height, first=0):
    return one_hot(lax.broadcasted_iota(jnp.int32, (height, row.shape[1]), 0) + first == row)


def activate(before):
    sig = 1.0 / (1.0 + jnp.exp(-before))
    return (before * sig).astype(BF16), sig * (1.0 + before * (1.0 - sig))


def normalise(output):
    centred = output - jnp.mean(output, axis=-1, keepdims=True)
    variance = jnp.mean(centred * centred, axis=-1, keepdims=True)
    rstd = lax.rsqrt(variance + 1e-05)
    return centred * rstd, rstd


def normalise_back(grad, xhat, rstd):
    first = jnp.mean(grad, axis=-1, keepdims=True)
    second = jnp.mean(grad * xhat, axis=-1, keepdims=True)
    return rstd * (grad - first - xhat * second)


def kernel(
    sizes,
    node_lat, edge_lat, node_ct, edge_ct,
    we_in, we_out, wn_in, wn_out,
    halo, sender, receiver,
    be_in, be_out, e_gain, e_shift, bn_in, bn_out, n_gain, n_shift,
    node_new, edge_new, edge_grad, node_grad,
    v_we_in, v_we_out, v_wn_in, v_wn_out, v_node,
    table, halo_buf, edges, edge_cts, node_cts,
    s_col, r_col, t_w, r_w, before, xhat_s, rstd_s, edge_s, node_s, dpre_s, grad_s,
    part, part_in, part_own, back_out, back_in, summed_s,
    w_sem, l_send, l_recv, r_send, r_recv, d_send, d_recv, b_send, b_recv,
):
    domains, rows, eb, nb, slots, width, tile, tiles = sizes
    p = lax.axis_index("dom")
    l = lax.axis_index("lat")
    o = 1 - l
    steps = eb // tile
    e_own = pl.ds(pl.multiple_of(l * eb, eb), eb)
    e_far = pl.ds(pl.multiple_of(o * eb, eb), eb)
    n_own = pl.ds(pl.multiple_of(l * nb, nb), nb)
    n_far = pl.ds(pl.multiple_of(o * nb, nb), nb)
    full = 2 * width

    barrier = pltpu.get_barrier_semaphore()

    def greet(d, c):
        pl.semaphore_signal(barrier, inc=1, device_id={"dom": lax.rem(p + d, domains)})
        return c

    lax.fori_loop(1, domains, greet, 0)
    pl.semaphore_signal(barrier, inc=1, device_id={"lat": o})

    local = [
        pltpu.make_async_copy(node_lat, v_node, w_sem.at[0]),
        pltpu.make_async_copy(we_in, v_we_in, w_sem.at[1]),
        pltpu.make_async_copy(node_lat, table.at[l, pl.ds(0, rows)], w_sem.at[2]),
        pltpu.make_async_copy(edge_lat.at[e_own], edges.at[l], w_sem.at[3]),
        pltpu.make_async_copy(we_out, v_we_out, w_sem.at[4]),
        pltpu.make_async_copy(wn_in, v_wn_in, w_sem.at[5]),
        pltpu.make_async_copy(wn_out, v_wn_out, w_sem.at[6]),
        pltpu.make_async_copy(node_ct.at[n_own], node_cts.at[l], w_sem.at[7]),
        pltpu.make_async_copy(edge_ct.at[e_own], edge_cts.at[l], w_sem.at[8]),
    ]
    for copy in local:
        copy.start()

    mine = pl.ds(pl.multiple_of(rows + p * slots, 16), slots)
    table[0, mine] = jnp.zeros((slots, width), BF16)
    table[1, mine] = jnp.zeros((slots, width), BF16)
    mine_back = pl.ds(pl.multiple_of(p * slots, 16), slots)
    back_in[mine_back] = jnp.zeros((slots, width), BF16)

    local[0].wait()
    for j in range(domains * slots // 128):
        col = column(halo[:, j * 128 : (j + 1) * 128])
        halo_buf[j * 128 : (j + 1) * 128] = mm(across(col, rows), v_node[...]).astype(BF16)

    pl.semaphore_wait(barrier, domains)

    def chunk(q):
        return pl.ds(pl.multiple_of(q * slots, 16), slots)

    def table_chunk(q):
        return pl.ds(pl.multiple_of(rows + q * slots, 16), slots)

    def dom_copy(q, source):
        return pltpu.make_async_remote_copy(
            src_ref=halo_buf.at[chunk(q)],
            dst_ref=table.at[l, table_chunk(source)],
            send_sem=d_send.at[q],
            recv_sem=d_recv.at[source],
            device_id={"dom": q},
        )

    def dom_start(d, c):
        dom_copy(lax.rem(p + d, domains), p).start()
        return c

    lax.fori_loop(1, domains, dom_start, 0)

    def lat_copy(src, dst, k):
        return pltpu.make_async_remote_copy(
            src_ref=src, dst_ref=dst, send_sem=l_send.at[k], recv_sem=l_recv.at[k], device_id={"lat": o}
        )

    to_lat = [
        lat_copy(node_lat, table.at[l, pl.ds(0, rows)], 0),
        lat_copy(edge_lat.at[e_far], edges.at[l], 1),
        lat_copy(node_ct.at[n_far], node_cts.at[l], 2),
        lat_copy(edge_ct.at[e_far], edge_cts.at[l], 3),
    ]
    for copy in to_lat:
        copy.start()

    def columns(i, c):
        at = pl.ds(pl.multiple_of(i * tile, tile), tile)
        lanes = pl.ds(pl.multiple_of(l * eb + i * tile, 128), tile)
        s_col[at] = column(sender[:, lanes])
        r_col[at] = column(receiver[:, lanes] - l * nb)
        return c

    lax.fori_loop(0, steps, columns, 0)

    local[1].wait()
    local[2].wait()
    to_lat[0].wait_recv()

    def both(ref, at):
        return jnp.concatenate([ref[0, at], ref[1, at]], axis=1)

    def halves(ref, at, value):
        ref[0, at] = value[:, :width]
        ref[1, at] = value[:, width:]

    w_e = v_we_in.at[pl.ds(0, full)]
    w_s = v_we_in.at[pl.ds(full, full)]
    w_r = v_we_in.at[pl.ds(2 * full, full)]
    wn_n = v_wn_in.at[pl.ds(0, full)]
    wn_s = v_wn_in.at[pl.ds(full, full)]

    node_full = both(table, n_own)
    r_w[...] = mm(node_full, w_r[...]).astype(BF16)

    def send_table(t, c):
        at = pl.ds(pl.multiple_of(t * rows, rows), rows)
        t_w[at] = mm(both(table, at), w_s[...]).astype(BF16)
        return c

    send_table(0, 0)
    if t_w.shape[0] > tiles * rows:
        t_w[tiles * rows :] = jnp.zeros((t_w.shape[0] - tiles * rows, full), BF16)

    local[3].wait()
    to_lat[1].wait_recv()

    def phase_a(i, c):
        at = pl.ds(pl.multiple_of(i * tile, tile), tile)
        value = mm(both(edges, at), w_e[...]) + mm(across(r_col[at], nb), r_w[...])
        before[at] = value + be_in[...]
        return c

    lax.fori_loop(0, steps, phase_a, 0)

    def relay_copy(q):
        return pltpu.make_async_remote_copy(
            src_ref=table.at[l, table_chunk(q)],
            dst_ref=table.at[l, table_chunk(q)],
            send_sem=r_send.at[q],
            recv_sem=r_recv.at[q],
            device_id={"lat": o},
        )

    def relay(d, c):
        q = lax.rem(p + domains - d, domains)
        dom_copy(q, q).wait_recv()
        relay_copy(q).start()
        return c

    lax.fori_loop(1, domains, relay, 0)

    def relayed(d, c):
        q = lax.rem(p + domains - d, domains)
        pltpu.make_async_remote_copy(
            src_ref=table.at[o, table_chunk(q)],
            dst_ref=table.at[o, table_chunk(q)],
            send_sem=r_send.at[q],
            recv_sem=r_recv.at[q],
            device_id={"lat": o},
        ).wait_recv()
        return c

    lax.fori_loop(1, domains, relayed, 0)
    lax.fori_loop(1, tiles, send_table, 0)
    local[4].wait()

    summed_s[...] = jnp.zeros_like(summed_s)

    def r_row(i):
        return receiver[:, pl.ds(pl.multiple_of(l * eb + i * tile, 128), tile)] - l * nb

    def phase_b(i, c):
        at = pl.ds(pl.multiple_of(i * tile, tile), tile)
        value = before[at] + mm(across(s_col[at], t_w.shape[0]), t_w[...])
        active, slope = activate(value)
        before[at] = slope
        xhat, rstd = normalise(mm(active, v_we_out[...]) + be_out[...])
        xhat_s[at] = xhat
        rstd_s[at] = jnp.broadcast_to(rstd, (tile, 128))
        fresh = (both(edges, at).astype(F32) + xhat * e_gain[...] + e_shift[...]).astype(BF16)
        halves(edge_s, at, fresh)
        summed_s[...] += mm(down(r_row(i), nb), fresh)
        return c

    lax.fori_loop(0, steps, phase_b, 0)

    edge_out = [
        pltpu.make_async_copy(edge_s.at[l], edge_new.at[e_own], w_sem.at[9]),
        lat_copy(edge_s.at[o], edge_new.at[e_own], 4),
    ]
    for copy in edge_out:
        copy.start()

    local[5].wait()
    local[6].wait()
    local[7].wait()
    to_lat[2].wait_recv()
    all_n = pl.ds(0, nb)
    node_full = both(table, n_own)
    active, slope = activate(
        mm(node_full, wn_n[...]) + mm(summed_s[...].astype(BF16), wn_s[...]) + bn_in[...]
    )
    xhat, rstd = normalise(mm(active, v_wn_out[...]) + bn_out[...])
    halves(
        node_s, all_n, (node_full.astype(F32) + xhat * n_gain[...] + n_shift[...]).astype(BF16)
    )
    node_out = [
        pltpu.make_async_copy(node_s.at[l], node_new.at[n_own], w_sem.at[10]),
        lat_copy(node_s.at[o], node_new.at[n_own], 5),
    ]
    for copy in node_out:
        copy.start()
    cot = both(node_cts, all_n).astype(F32)
    d_out = normalise_back(cot * n_gain[...], xhat, rstd).astype(BF16)
    d_before = (mm_t(d_out, v_wn_out[...]).astype(BF16).astype(F32) * slope).astype(BF16)
    node_part = cot + mm_t(d_before, wn_n[...]).astype(BF16).astype(F32)
    summed_s[...] = node_part
    r_w[...] = mm_t(d_before, wn_s[...]).astype(BF16)

    local[8].wait()
    to_lat[3].wait_recv()

    def phase_c(i, c):
        at = pl.ds(pl.multiple_of(i * tile, tile), tile)
        gathered = mm(across(r_col[at], nb), r_w[...])
        g = (both(edge_cts, at).astype(F32) + gathered).astype(BF16).astype(F32)
        rstd = rstd_s[at][:, :1]
        d_out = normalise_back(g * e_gain[...], xhat_s[at], rstd).astype(BF16)
        d_before = (mm_t(d_out, v_we_out[...]).astype(BF16).astype(F32) * before[at]).astype(BF16)
        dpre_s[at] = d_before
        halves(grad_s, at, (g + mm_t(d_before, w_e[...])).astype(BF16))
        return c

    lax.fori_loop(0, steps, phase_c, 0)

    row_lanes = pl.ds(pl.multiple_of(l * eb, 128), eb)

    def slot_part(t):
        hot = down(sender[:, row_lanes], rows, t * rows)
        return mm_t(mm(hot, dpre_s[...]).astype(BF16), w_s[...])

    def part_copy(t):
        at = pl.ds(pl.multiple_of(t * rows, rows), rows)
        return lat_copy(part.at[o, at], part_in.at[at], 7 + t)

    def parts(t, c):
        at = pl.ds(pl.multiple_of(t * rows, rows), rows)
        halves(part, at, slot_part(t).astype(BF16))
        part_copy(t).start()
        return c

    lax.fori_loop(1, tiles, parts, 0)

    def back_copy(q, source):
        return pltpu.make_async_remote_copy(
            src_ref=back_out.at[chunk(q)],
            dst_ref=back_in.at[chunk(source)],
            send_sem=b_send.at[q],
            recv_sem=b_recv.at[source],
            device_id={"dom": q},
        )

    per = rows // slots

    def back(t, c):
        at = pl.ds(pl.multiple_of(t * rows, rows), rows)
        part_copy(t).wait_recv()
        out = pl.ds(pl.multiple_of((t - 1) * rows, rows), rows)
        back_out[out] = (part[l, at].astype(F32) + part_in[at].astype(F32)).astype(BF16)
        for k in range(per):
            q = (t - 1) * per + k

            @pl.when(q != p)
            def _():
                back_copy(q, p).start()

        return c

    lax.fori_loop(1, tiles, back, 0)

    first = pl.ds(0, rows)
    halves(part_own, first, slot_part(0))
    hot = down(receiver[:, row_lanes] - l * nb, nb)
    node_part = summed_s[...] + mm_t(mm(hot, dpre_s[...]).astype(BF16), w_r[...])
    part_own[0, n_own] += node_part[:, :width]
    part_own[1, n_own] += node_part[:, width:]
    part[o, first] = part_own[o].astype(BF16)
    part_copy(0).start()

    grad_out = [
        pltpu.make_async_copy(grad_s.at[l], edge_grad.at[e_own], w_sem.at[11]),
        lat_copy(grad_s.at[o], edge_grad.at[e_own], 6),
    ]
    for copy in grad_out:
        copy.start()

    part_copy(0).wait_recv()

    def arrived(d, c):
        q = lax.rem(p + domains - d, domains)
        back_copy(q, q).wait_recv()
        return c

    lax.fori_loop(1, domains, arrived, 0)
    node_grad[...] = (
        part_own[l] + part_in[first].astype(F32) + mm(down(halo[...], rows), back_in[...])
    )

    def sent(d, c):
        q = lax.rem(p + d, domains)
        dom_copy(q, p).wait_send()
        relay_copy(q).wait_send()
        back_copy(q, p).wait_send()
        return c

    lax.fori_loop(1, domains, sent, 0)

    def parts_sent(t, c):
        part_copy(t).wait_send()
        return c

    lax.fori_loop(0, tiles, parts_sent, 0)
    for copy in to_lat:
        copy.wait_send()
    for pair in (edge_out, node_out, grad_out):
        pair[0].wait()
        pair[1].wait()


def on_device(
    node_lat, edge_lat, halo_rows, edge_sender, edge_receiver,
    edge_w_in, edge_b_in, edge_w_out, edge_b_out, edge_gain, edge_shift,
    node_w_in, node_b_in, node_w_out, node_b_out, node_gain, node_shift,
    node_ct, edge_ct,
):
    domains = lax.axis_size("dom")
    rows, width = node_lat.shape
    edge_rows = edge_lat.shape[0]
    slots = halo_rows.shape[2]
    eb, nb = edge_rows // 2, rows // 2
    full = 2 * width
    units = edge_w_out.shape[0]
    tile = 256
    tiles = 1 + domains * slots // rows
    slot_rows = tiles * rows
    depth = -(-slot_rows // 256) * 256
    halo = lax.dynamic_index_in_dim(halo_rows, lax.axis_index("dom"), 0, keepdims=False)
    halo = halo.reshape(1, domains * slots)
    any_spec = pl.BlockSpec(memory_space=pl.ANY)
    vmem = pl.BlockSpec(memory_space=pltpu.VMEM)
    dma = pltpu.SemaphoreType.DMA
    scratch = [
        pltpu.VMEM(edge_w_in.shape, BF16),
        pltpu.VMEM(edge_w_out.shape, BF16),
        pltpu.VMEM(node_w_in.shape, BF16),
        pltpu.VMEM(node_w_out.shape, BF16),
        pltpu.VMEM((rows, width), BF16),
        pltpu.VMEM((2, slot_rows, width), BF16),
        pltpu.VMEM((domains * slots, width), BF16),
        pltpu.VMEM((2, eb, width), BF16),
        pltpu.VMEM((2, eb, width), BF16),
        pltpu.VMEM((2, nb, width), BF16),
        pltpu.VMEM((eb, 128), jnp.int32),
        pltpu.VMEM((eb, 128), jnp.int32),
        pltpu.VMEM((depth, units), BF16),
        pltpu.VMEM((nb, units), BF16),
        pltpu.VMEM((eb, units), F32),
        pltpu.VMEM((eb, full), F32),
        pltpu.VMEM((eb, 128), F32),
        pltpu.VMEM((2, eb, width), BF16),
        pltpu.VMEM((2, nb, width), BF16),
        pltpu.VMEM((eb, units), BF16),
        pltpu.VMEM((2, eb, width), BF16),
        pltpu.VMEM((2, slot_rows, width), BF16),
        pltpu.VMEM((slot_rows, width), BF16),
        pltpu.VMEM((2, rows, width), F32),
        pltpu.VMEM((domains * slots, width), BF16),
        pltpu.VMEM((domains * slots, width), BF16),
        pltpu.VMEM((nb, full), F32),
        dma((12,)),
        dma((7 + tiles,)),
        dma((7 + tiles,)),
    ] + [dma((domains,)) for _ in range(6)]
    sizes = (domains, rows, eb, nb, slots, width, tile, tiles)

    def line(x):
        return x.reshape(1, -1)

    node_new, edge_new, edge_grad, node_grad = pl.pallas_call(
        functools.partial(kernel, sizes),
        out_shape=(
            jax.ShapeDtypeStruct((rows, width), BF16),
            jax.ShapeDtypeStruct((edge_rows, width), BF16),
            jax.ShapeDtypeStruct((edge_rows, width), BF16),
            jax.ShapeDtypeStruct((rows, width), F32),
        ),
        in_specs=[any_spec] * 8 + [vmem] * 11,
        out_specs=(any_spec, any_spec, any_spec, vmem),
        scratch_shapes=scratch,
        compiler_params=pltpu.CompilerParams(
            collective_id=0, has_side_effects=True, vmem_limit_bytes=48 * 1024 * 1024
        ),
    )(
        node_lat, edge_lat, node_ct, edge_ct,
        edge_w_in, edge_w_out, node_w_in, node_w_out,
        halo, line(edge_sender), line(edge_receiver),
        line(edge_b_in), line(edge_b_out), line(edge_gain), line(edge_shift),
        line(node_b_in), line(node_b_out), line(node_gain), line(node_shift),
    )
    return (node_new, edge_new, node_grad, edge_grad.astype(F32))


def solution(mesh):
    many = P(("ens", "dom"), "lat")
    return jax.shard_map(
        on_device,
        mesh=mesh,
        in_specs=(many, many, P("ens", None, None), P(("ens", "dom")), P(("ens", "dom")))
        + (P(),) * 12
        + (many, many),
        out_specs=(many,) * 4,
        check_vma=False,
    )
```

```python
import functools

import jax
import jax.numpy as jnp
from jax import lax
from jax.experimental import pallas as pl
from jax.experimental.pallas import tpu as pltpu
from jax.sharding import PartitionSpec as P

F32 = jnp.float32
BF16 = jnp.bfloat16
UNROLL = True


def mm(a, b):
    return jnp.dot(a, b, preferred_element_type=F32)


def mm_t(a, b):
    return lax.dot_general(a, b, (((1,), (1,)), ((), ())), preferred_element_type=F32)


def one_hot(match):
    return jnp.where(match, 1.0, 0.0).astype(BF16)


def column(row):
    return jnp.broadcast_to(row, (128, row.shape[1])).T


def across(col, depth):
    return one_hot(lax.broadcasted_iota(jnp.int32, (col.shape[0], depth), 1) == col[:, :1])


def down(row, height, first=0):
    return one_hot(lax.broadcasted_iota(jnp.int32, (height, row.shape[1]), 0) + first == row)


def activate(before):
    sig = 0.5 + 0.5 * jnp.tanh(0.5 * before)
    return (before * sig).astype(BF16), sig * (1.0 + before * (1.0 - sig))


def normalise(output):
    centred = output - jnp.mean(output, axis=-1, keepdims=True)
    variance = jnp.mean(centred * centred, axis=-1, keepdims=True)
    rstd = lax.rsqrt(variance + 1e-05)
    return centred * rstd, rstd


def normalise_back(grad, xhat, rstd):
    first = jnp.mean(grad, axis=-1, keepdims=True)
    second = jnp.mean(grad * xhat, axis=-1, keepdims=True)
    return rstd * (grad - first - xhat * second)


def kernel(
    sizes,
    node_lat, edge_lat, node_ct, edge_ct,
    we_in, we_out, wn_in, wn_out,
    halo_h, sender_h, receiver_h,
    h0, h1, h2, h3, h4, h5, h6, h7,
    node_new, edge_new, edge_grad, node_grad,
    halo, sender_v, receiver_v, sender, receiver,
    be_in, be_out, e_gain, e_shift, bn_in, bn_out, n_gain, n_shift,
    v_we_in, v_we_out, v_wn_in, v_wn_out, v_node,
    table, halo_buf, edges, edge_cts, node_cts,
    s_col, r_col, t_w, own_w, r_w, before, xhat_s, rstd_s, edge_s, node_s, dpre_s, grad_s,
    part, part_in, part_own, back_out, back_in, summed_s,
    i_sem, w_sem, l_send, l_recv, r_send, r_recv, d_send, d_recv, b_send, b_recv,
):
    domains, rows, eb, nb, slots, width, tile, tiles = sizes
    p = lax.axis_index("dom")
    l = lax.axis_index("lat")
    o = 1 - l
    steps = eb // tile
    e_own = pl.ds(pl.multiple_of(l * eb, eb), eb)
    e_far = pl.ds(pl.multiple_of(o * eb, eb), eb)
    n_own = pl.ds(pl.multiple_of(l * nb, nb), nb)
    n_far = pl.ds(pl.multiple_of(o * nb, nb), nb)
    full = 2 * width

    small = [
        pltpu.make_async_copy(src, dst, i_sem.at[k])
        for k, (src, dst) in enumerate(
            (
                (halo_h, halo), (sender_h, sender_v), (receiver_h, receiver_v),
                (h0, be_in), (h1, be_out), (h2, e_gain), (h3, e_shift),
                (h4, bn_in), (h5, bn_out), (h6, n_gain), (h7, n_shift),
            )
        )
    ]
    barrier = pltpu.get_barrier_semaphore()

    def greet(d, c):
        pl.semaphore_signal(barrier, inc=1, device_id={"dom": lax.rem(p + d, domains)})
        return c

    lax.fori_loop(1, domains, greet, 0)
    pl.semaphore_signal(barrier, inc=1, device_id={"lat": o})

    local = [
        pltpu.make_async_copy(node_lat, v_node, w_sem.at[0]),
        pltpu.make_async_copy(we_in, v_we_in, w_sem.at[1]),
        pltpu.make_async_copy(node_lat, table.at[l, pl.ds(0, rows)], w_sem.at[2]),
        pltpu.make_async_copy(edge_lat.at[e_own], edges.at[l], w_sem.at[3]),
        pltpu.make_async_copy(we_out, v_we_out, w_sem.at[4]),
        pltpu.make_async_copy(wn_in, v_wn_in, w_sem.at[5]),
        pltpu.make_async_copy(wn_out, v_wn_out, w_sem.at[6]),
        pltpu.make_async_copy(node_ct.at[n_own], node_cts.at[l], w_sem.at[7]),
        pltpu.make_async_copy(edge_ct.at[e_own], edge_cts.at[l], w_sem.at[8]),
    ]
    small[0].start()
    local[0].start()
    for copy in small[1:] + local[1:]:
        copy.start()

    mine = pl.ds(pl.multiple_of(rows + p * slots, 16), slots)
    table[0, mine] = jnp.zeros((slots, width), BF16)
    table[1, mine] = jnp.zeros((slots, width), BF16)
    mine_back = pl.ds(pl.multiple_of(p * slots, 16), slots)
    back_in[mine_back] = jnp.zeros((slots, width), BF16)

    small[0].wait()
    local[0].wait()
    for j in range(domains * slots // 128):
        col = column(halo[:, j * 128 : (j + 1) * 128])
        halo_buf[j * 128 : (j + 1) * 128] = mm(across(col, rows), v_node[...]).astype(BF16)

    pl.semaphore_wait(barrier, domains)

    def chunk(q):
        return pl.ds(pl.multiple_of(q * slots, 16), slots)

    def table_chunk(q):
        return pl.ds(pl.multiple_of(rows + q * slots, 16), slots)

    def dom_copy(q, source):
        return pltpu.make_async_remote_copy(
            src_ref=halo_buf.at[chunk(q)],
            dst_ref=table.at[l, table_chunk(source)],
            send_sem=d_send.at[q],
            recv_sem=d_recv.at[source],
            device_id={"dom": q},
        )

    def dom_start(d, c):
        dom_copy(lax.rem(p + d, domains), p).start()
        return c

    lax.fori_loop(1, domains, dom_start, 0)

    def lat_copy(src, dst, k):
        return pltpu.make_async_remote_copy(
            src_ref=src, dst_ref=dst, send_sem=l_send.at[k], recv_sem=l_recv.at[k], device_id={"lat": o}
        )

    to_lat = [
        lat_copy(node_lat, table.at[l, pl.ds(0, rows)], 0),
        lat_copy(edge_lat.at[e_far], edges.at[l], 1),
        lat_copy(node_ct.at[n_far], node_cts.at[l], 2),
        lat_copy(edge_ct.at[e_far], edge_cts.at[l], 3),
    ]
    for copy in to_lat:
        copy.start()

    small[1].wait()
    small[2].wait()
    groups = eb // 128
    for j in range(groups):
        at = pl.ds(j * 128, 128)
        sender[:, at] = sender_v[pl.ds(l * groups + j, 1), :]
        receiver[:, at] = receiver_v[pl.ds(l * groups + j, 1), :] - l * nb
        s_col[at] = column(sender[:, at])
        r_col[at] = column(receiver[:, at])
    for copy in small[3:]:
        copy.wait()

    local[1].wait()
    local[2].wait()
    to_lat[0].wait_recv()

    def both(ref, at):
        return jnp.concatenate([ref[0, at], ref[1, at]], axis=1)

    def halves(ref, at, value):
        ref[0, at] = value[:, :width]
        ref[1, at] = value[:, width:]

    w_e = v_we_in.at[pl.ds(0, full)]
    w_s = v_we_in.at[pl.ds(full, full)]
    w_r = v_we_in.at[pl.ds(2 * full, full)]
    wn_n = v_wn_in.at[pl.ds(0, full)]
    wn_s = v_wn_in.at[pl.ds(full, full)]

    node_full = both(table, n_own)
    near = own_w.shape[0]
    own_w[rows : rows + nb] = mm(node_full, w_r[...]).astype(BF16)
    own_w[:rows] = mm(both(table, pl.ds(0, rows)), w_s[...]).astype(BF16)
    if near > rows + nb:
        own_w[rows + nb :] = jnp.zeros((near - rows - nb, full), BF16)

    def send_table(t, c):
        at = pl.ds(pl.multiple_of(t * rows, rows), rows)
        to = pl.ds(pl.multiple_of((t - 1) * rows, rows), rows)
        t_w[to] = mm(both(table, at), w_s[...]).astype(BF16)
        return c

    if t_w.shape[0] > (tiles - 1) * rows:
        t_w[(tiles - 1) * rows :] = jnp.zeros((t_w.shape[0] - (tiles - 1) * rows, full), BF16)

    local[3].wait()
    to_lat[1].wait_recv()

    def phase_a(i, c):
        at = pl.ds(pl.multiple_of(i * tile, tile), tile)
        lane = lax.broadcasted_iota(jnp.int32, (tile, near), 1)
        from_own = jnp.where(s_col[at][:, :1] < rows, s_col[at][:, :1], -1)
        hot = one_hot((lane == from_own) | (lane == r_col[at][:, :1] + rows))
        value = mm(both(edges, at), w_e[...]) + mm(hot, own_w[...])
        before[at] = value + be_in[...]
        return c

    lax.fori_loop(0, steps, phase_a, 0, unroll=UNROLL)

    def relay_copy(q):
        return pltpu.make_async_remote_copy(
            src_ref=table.at[l, table_chunk(q)],
            dst_ref=table.at[l, table_chunk(q)],
            send_sem=r_send.at[q],
            recv_sem=r_recv.at[q],
            device_id={"lat": o},
        )

    def relay(d, c):
        q = lax.rem(p + domains - d, domains)
        dom_copy(q, q).wait_recv()
        relay_copy(q).start()
        return c

    lax.fori_loop(1, domains, relay, 0)

    def relayed(d, c):
        q = lax.rem(p + domains - d, domains)
        pltpu.make_async_remote_copy(
            src_ref=table.at[o, table_chunk(q)],
            dst_ref=table.at[o, table_chunk(q)],
            send_sem=r_send.at[q],
            recv_sem=r_recv.at[q],
            device_id={"lat": o},
        ).wait_recv()
        return c

    lax.fori_loop(1, domains, relayed, 0)
    lax.fori_loop(1, tiles, send_table, 0)
    local[4].wait()

    summed_s[...] = jnp.zeros_like(summed_s)

    def r_row(i):
        return receiver[:, pl.ds(pl.multiple_of(i * tile, 128), tile)]

    def phase_b(i, c):
        at = pl.ds(pl.multiple_of(i * tile, tile), tile)
        value = before[at] + mm(across(s_col[at] - rows, t_w.shape[0]), t_w[...])
        active, slope = activate(value)
        before[at] = slope
        xhat, rstd = normalise(mm(active, v_we_out[...]) + be_out[...])
        xhat_s[at] = xhat
        rstd_s[at] = jnp.broadcast_to(rstd, (tile, 128))
        fresh = (both(edges, at).astype(F32) + xhat * e_gain[...] + e_shift[...]).astype(BF16)
        halves(edge_s, at, fresh)
        summed_s[...] += mm(down(r_row(i), nb), fresh)
        return c

    lax.fori_loop(0, steps, phase_b, 0, unroll=UNROLL)

    edge_out = [
        pltpu.make_async_copy(edge_s.at[l], edge_new.at[e_own], w_sem.at[9]),
        lat_copy(edge_s.at[o], edge_new.at[e_own], 4),
    ]
    for copy in edge_out:
        copy.start()

    local[5].wait()
    local[6].wait()
    local[7].wait()
    to_lat[2].wait_recv()
    all_n = pl.ds(0, nb)
    node_full = both(table, n_own)
    active, slope = activate(
        mm(node_full, wn_n[...]) + mm(summed_s[...].astype(BF16), wn_s[...]) + bn_in[...]
    )
    xhat, rstd = normalise(mm(active, v_wn_out[...]) + bn_out[...])
    halves(
        node_s, all_n, (node_full.astype(F32) + xhat * n_gain[...] + n_shift[...]).astype(BF16)
    )
    node_out = [
        pltpu.make_async_copy(node_s.at[l], node_new.at[n_own], w_sem.at[10]),
        lat_copy(node_s.at[o], node_new.at[n_own], 5),
    ]
    for copy in node_out:
        copy.start()
    cot = both(node_cts, all_n).astype(F32)
    d_out = normalise_back(cot * n_gain[...], xhat, rstd).astype(BF16)
    d_before = (mm_t(d_out, v_wn_out[...]).astype(BF16).astype(F32) * slope).astype(BF16)
    node_part = cot + mm_t(d_before, wn_n[...]).astype(BF16).astype(F32)
    summed_s[...] = node_part
    r_w[...] = mm_t(d_before, wn_s[...]).astype(BF16)

    local[8].wait()
    to_lat[3].wait_recv()

    def phase_c(i, c):
        at = pl.ds(pl.multiple_of(i * tile, tile), tile)
        gathered = mm(across(r_col[at], nb), r_w[...])
        g = (both(edge_cts, at).astype(F32) + gathered).astype(BF16)
        halves(edge_cts, at, g)
        g = g.astype(F32)
        rstd = rstd_s[at][:, :1]
        d_out = normalise_back(g * e_gain[...], xhat_s[at], rstd).astype(BF16)
        d_before = (mm_t(d_out, v_we_out[...]).astype(BF16).astype(F32) * before[at]).astype(BF16)
        dpre_s[at] = d_before
        return c

    lax.fori_loop(0, steps, phase_c, 0, unroll=UNROLL)

    def slot_part(t):
        hot = down(sender[...], rows, t * rows)
        return mm_t(mm(hot, dpre_s[...]).astype(BF16), w_s[...])

    def part_copy(t):
        at = pl.ds(pl.multiple_of(t * rows, rows), rows)
        return lat_copy(part.at[o, at], part_in.at[at], 7 + t)

    def parts(t, c):
        at = pl.ds(pl.multiple_of(t * rows, rows), rows)
        halves(part, at, slot_part(t).astype(BF16))
        part_copy(t).start()
        return c

    lax.fori_loop(1, tiles, parts, 0)

    def back_copy(q, source):
        return pltpu.make_async_remote_copy(
            src_ref=back_out.at[chunk(q)],
            dst_ref=back_in.at[chunk(source)],
            send_sem=b_send.at[q],
            recv_sem=b_recv.at[source],
            device_id={"dom": q},
        )

    per = rows // slots

    def back(t, c):
        at = pl.ds(pl.multiple_of(t * rows, rows), rows)
        part_copy(t).wait_recv()
        out = pl.ds(pl.multiple_of((t - 1) * rows, rows), rows)
        back_out[out] = (part[l, at].astype(F32) + part_in[at].astype(F32)).astype(BF16)
        for k in range(per):
            q = (t - 1) * per + k

            @pl.when(q != p)
            def _():
                back_copy(q, p).start()

        return c

    lax.fori_loop(1, tiles, back, 0)

    first = pl.ds(0, rows)
    halves(part_own, first, slot_part(0))
    hot = down(receiver[...], nb)
    node_part = summed_s[...] + mm_t(mm(hot, dpre_s[...]).astype(BF16), w_r[...])
    part_own[0, n_own] += node_part[:, :width]
    part_own[1, n_own] += node_part[:, width:]
    part[o, first] = part_own[o].astype(BF16)
    part_copy(0).start()

    def phase_d(i, c):
        at = pl.ds(pl.multiple_of(i * tile, tile), tile)
        g = both(edge_cts, at).astype(F32)
        halves(grad_s, at, (g + mm_t(dpre_s[at], w_e[...])).astype(BF16))
        return c

    lax.fori_loop(0, steps, phase_d, 0, unroll=UNROLL)

    grad_out = [
        pltpu.make_async_copy(grad_s.at[l], edge_grad.at[e_own], w_sem.at[11]),
        lat_copy(grad_s.at[o], edge_grad.at[e_own], 6),
    ]
    for copy in grad_out:
        copy.start()

    part_copy(0).wait_recv()

    def arrived(d, c):
        q = lax.rem(p + domains - d, domains)
        back_copy(q, q).wait_recv()
        return c

    lax.fori_loop(1, domains, arrived, 0)
    node_grad[...] = (
        part_own[l] + part_in[first].astype(F32) + mm(down(halo[...], rows), back_in[...])
    )

    def sent(d, c):
        q = lax.rem(p + d, domains)
        dom_copy(q, p).wait_send()
        relay_copy(q).wait_send()
        back_copy(q, p).wait_send()
        return c

    lax.fori_loop(1, domains, sent, 0)

    def parts_sent(t, c):
        part_copy(t).wait_send()
        return c

    lax.fori_loop(0, tiles, parts_sent, 0)
    for copy in to_lat:
        copy.wait_send()
    for pair in (edge_out, node_out, grad_out):
        pair[0].wait()
        pair[1].wait()


def on_device(
    node_lat, edge_lat, halo_rows, edge_sender, edge_receiver,
    edge_w_in, edge_b_in, edge_w_out, edge_b_out, edge_gain, edge_shift,
    node_w_in, node_b_in, node_w_out, node_b_out, node_gain, node_shift,
    node_ct, edge_ct,
):
    domains = lax.axis_size("dom")
    rows, width = node_lat.shape
    edge_rows = edge_lat.shape[0]
    slots = halo_rows.shape[2]
    eb, nb = edge_rows // 2, rows // 2
    full = 2 * width
    units = edge_w_out.shape[0]
    tile = 256
    tiles = 1 + domains * slots // rows
    slot_rows = tiles * rows
    depth = -(-(slot_rows - rows) // 128) * 128
    near = -(-(rows + nb) // 256) * 256
    halo = lax.dynamic_index_in_dim(halo_rows, lax.axis_index("dom"), 0, keepdims=False)
    halo = halo.reshape(1, domains * slots)
    any_spec = pl.BlockSpec(memory_space=pl.ANY)
    vmem = pl.BlockSpec(memory_space=pltpu.VMEM)
    dma = pltpu.SemaphoreType.DMA
    scratch = [
        pltpu.VMEM((1, domains * slots), jnp.int32),
        pltpu.VMEM((edge_rows // 128, 128), jnp.int32),
        pltpu.VMEM((edge_rows // 128, 128), jnp.int32),
        pltpu.VMEM((1, eb), jnp.int32),
        pltpu.VMEM((1, eb), jnp.int32),
    ] + [pltpu.VMEM((1, full), F32) for _ in range(8)] + [
        pltpu.VMEM(edge_w_in.shape, BF16),
        pltpu.VMEM(edge_w_out.shape, BF16),
        pltpu.VMEM(node_w_in.shape, BF16),
        pltpu.VMEM(node_w_out.shape, BF16),
        pltpu.VMEM((rows, width), BF16),
        pltpu.VMEM((2, slot_rows, width), BF16),
        pltpu.VMEM((domains * slots, width), BF16),
        pltpu.VMEM((2, eb, width), BF16),
        pltpu.VMEM((2, eb, width), BF16),
        pltpu.VMEM((2, nb, width), BF16),
        pltpu.VMEM((eb, 128), jnp.int32),
        pltpu.VMEM((eb, 128), jnp.int32),
        pltpu.VMEM((depth, units), BF16),
        pltpu.VMEM((near, units), BF16),
        pltpu.VMEM((nb, units), BF16),
        pltpu.VMEM((eb, units), F32),
        pltpu.VMEM((eb, full), F32),
        pltpu.VMEM((eb, 128), F32),
        pltpu.VMEM((2, eb, width), BF16),
        pltpu.VMEM((2, nb, width), BF16),
        pltpu.VMEM((eb, units), BF16),
        pltpu.VMEM((2, eb, width), BF16),
        pltpu.VMEM((2, slot_rows, width), BF16),
        pltpu.VMEM((slot_rows, width), BF16),
        pltpu.VMEM((2, rows, width), F32),
        pltpu.VMEM((domains * slots, width), BF16),
        pltpu.VMEM((domains * slots, width), BF16),
        pltpu.VMEM((nb, full), F32),
        dma((11,)),
        dma((12,)),
        dma((7 + tiles,)),
        dma((7 + tiles,)),
    ] + [dma((domains,)) for _ in range(6)]
    sizes = (domains, rows, eb, nb, slots, width, tile, tiles)

    def line(x):
        return x.reshape(1, -1)

    node_new, edge_new, edge_grad, node_grad = pl.pallas_call(
        functools.partial(kernel, sizes),
        out_shape=(
            jax.ShapeDtypeStruct((rows, width), BF16),
            jax.ShapeDtypeStruct((edge_rows, width), BF16),
            jax.ShapeDtypeStruct((edge_rows, width), BF16),
            jax.ShapeDtypeStruct((rows, width), F32),
        ),
        in_specs=[any_spec] * 19,
        out_specs=(any_spec, any_spec, any_spec, vmem),
        scratch_shapes=scratch,
        compiler_params=pltpu.CompilerParams(
            collective_id=0, has_side_effects=True, vmem_limit_bytes=60 * 1024 * 1024
        ),
    )(
        node_lat, edge_lat, node_ct, edge_ct,
        edge_w_in, edge_w_out, node_w_in, node_w_out,
        halo, edge_sender.reshape(-1, 128), edge_receiver.reshape(-1, 128),
        line(edge_b_in), line(edge_b_out), line(edge_gain), line(edge_shift),
        line(node_b_in), line(node_b_out), line(node_gain), line(node_shift),
    )
    return (node_new, edge_new, node_grad, edge_grad.astype(F32))


def solution(mesh):
    many = P(("ens", "dom"), "lat")
    return jax.shard_map(
        on_device,
        mesh=mesh,
        in_specs=(many, many, P("ens", None, None), P(("ens", "dom")), P(("ens", "dom")))
        + (P(),) * 12
        + (many, many),
        out_specs=(many,) * 4,
        check_vma=False,
    )
```
